32 devices in a mesh: row: 2 (over y), col: 4 (over z), depth: 4 (over x, core).
Axes of the slice: x: 2, y: 2, z: 4, core: 2. Of those that a mesh axis runs over, the one named last changes fastest.
Arguments:
- a_tiles: bfloat16 [2, 4, 4, 4, 128, 128], P('row', 'col', 'depth'), may hold values from -0.625 to 0.625
- pair_lists: int32 [2, 4, 4, 4, 2, 4, 12], P('row', 'col', 'depth'), may hold values from 0 to 7, as said below
Outputs:
- product_blocks: float32 [2, 4, 12, 128, 128], P('row', 'col', 'depth')
The draws below stay inside these ranges and needn't reach their ends.
Inputs may be any that keep to these rules, and one draw needn't show every extreme that they name: pair_lists[..., 0, m, o] is a left slot below 4, or 4 for an empty pair slot; the live pairs of a product block come first; pair_lists[..., 1, m, o] is a slot of the right panel.
All inputs are finite; a program needn't handle non-finite values.
Results may differ from the reference program's by a relative error of at most 0.0003.
Values may be sent and summed in bfloat16 or wider, within the bound.
No kernel may reach another device: no remote copies, remote signals or barrier semaphores. Data moves between devices by JAX's collectives and lax.ppermute only.
A program may use at most 64 MiB of HBM per device.

```python
import jax
import jax.numpy as jnp
from jax import lax

BLOCK = 128
S = 4
PAIRS = 4
SHIFTS = 4
RIGHT_SLOTS = 8
OUT_TOT = 12
N_ROW = 2
N_COL = 4
N_DEPTH = 4


def draw_pair_lists(key, part):
    base_key = jax.random.fold_in(key, 7)
    key_count, key_load, key_left, key_right = jax.random.split(base_key, 4)
    head_shape = (N_ROW, N_COL, N_DEPTH, SHIFTS)
    live_count = jax.random.randint(key_count, head_shape + (1, OUT_TOT), 1, PAIRS)
    device_load = jax.random.randint(key_load, (N_ROW, N_COL, N_DEPTH, 1, 1, 1), 0, 2)
    live_count = jnp.minimum(live_count + device_load, PAIRS)
    live_count = live_count.at[:, :, :, :, 0, 0].set(1)
    live_count = live_count.at[:, :, :, :, 0, 1].set(PAIRS)
    position = jnp.arange(PAIRS, dtype=jnp.int32).reshape(PAIRS, 1)
    left_slot = jax.random.randint(key_left, head_shape + (PAIRS, OUT_TOT), 0, S)
    left_slot = jnp.where(position < live_count, left_slot, S)
    right_slot = jax.random.randint(key_right, head_shape + (PAIRS, OUT_TOT), 0, RIGHT_SLOTS)
    right_slot = right_slot.at[:, :, :, 0, 0, 0].set(RIGHT_SLOTS - 1)
    return jnp.stack([left_slot, right_slot], axis=4).astype(jnp.int32)


def levels(stream_key, extent, cuts, least, high):
    loudness, own = 1.0, jax.random.fold_in(stream_key, 6)
    for dim, parts in cuts:
        heights = jnp.exp(jax.random.uniform(jax.random.fold_in(own, dim), (parts,), jnp.float32, least / len(cuts), high / len(cuts)))
        loudness = loudness * jnp.repeat(heights, extent[dim] // parts).reshape([-1 if axis == dim else 1 for axis in range(len(extent))])
    return loudness


def noise(stream_key, dims, width, bound, cuts=(), kind=jnp.bfloat16):
    level = levels(stream_key, dims, cuts, -0.22, 0.18) if cuts else 1.0
    result = jax.random.normal(stream_key, dims, jnp.float32) * width * level
    return jnp.minimum(jnp.maximum(result, -bound), bound).astype(kind)


def setup_inputs(seed: int = 0) -> dict:
    seeds = jax.random.split(jax.random.key(seed), 3)
    return {
        "a_tiles": noise(seeds[0], (N_ROW, N_COL, N_DEPTH, S, BLOCK, BLOCK), 0.1, 0.625, ((0, 2), (1, 4), (2, 4))),
        "pair_lists": draw_pair_lists(jax.random.fold_in(seeds[2], 71), 0),
    }


def reference(a_tiles, pair_lists):
    grid_rows = a_tiles.shape[0]
    grid_cols = a_tiles.shape[1]
    layers = a_tiles.shape[2]
    block_width = a_tiles.shape[4]
    out_total = pair_lists.shape[6]
    zero_block = jnp.zeros((grid_cols, 1, block_width, block_width), a_tiles.dtype)
    shift_index = jnp.arange(grid_cols, dtype=jnp.int32)

    def product_cell(flat_index):
        row_index = flat_index // grid_cols
        col_index = flat_index % grid_cols

        def add_layer(layer_index, running):
            row_tiles = a_tiles[row_index, :, layer_index]
            padded_rows = jnp.concatenate([row_tiles, zero_block], axis=1)
            col_tiles = a_tiles[:, col_index, layer_index].reshape(-1, block_width, block_width)
            pair_table = pair_lists[row_index, col_index, layer_index]
            sources = ((col_index - shift_index) % grid_cols).astype(jnp.int32)
            chosen = padded_rows[sources[:, None, None], pair_table[:, 0]]
            partner = col_tiles[pair_table[:, 1]]
            return running + jnp.einsum("smoik,smojk->oij", chosen.astype(jnp.float32), partner.astype(jnp.float32), precision=lax.Precision.HIGHEST)

        return lax.fori_loop(0, layers, add_layer, jnp.zeros((out_total, block_width, block_width), jnp.float32))

    blocks = lax.map(product_cell, jnp.arange(grid_rows * grid_cols, dtype=jnp.int32))
    return blocks.reshape(grid_rows, grid_cols, out_total, block_width, block_width)
```

```python
import functools

import jax
import jax.numpy as jnp
from jax import lax
from jax.experimental import pallas as pl
from jax.experimental.pallas import tpu as pltpu
from jax.sharding import PartitionSpec as P

VMEM = pl.BlockSpec(memory_space=pltpu.VMEM)
SMEM = pl.BlockSpec(memory_space=pltpu.SMEM)


def exchange(block, axis, distance):
    size = lax.axis_size(axis)
    return lax.ppermute(block, axis, [(i, i ^ distance) for i in range(size)])


def bits_down(size):
    return [1 << b for b in reversed(range(size.bit_length() - 1))]


def table_kernel(sizes, lists, table):
    cols, depths, slots, pairs, outs = sizes
    row, col, layer = (lax.axis_index(name) for name in ("row", "col", "depth"))
    share = outs // depths
    zero_slot = lax.axis_size("row") * slots

    def at(step, carry):
        hop, group = step // depths, step % depths
        shift = lax.rem(col - (col ^ hop) + cols, cols)
        for i in range(share):
            out = (layer ^ group) * share + i
            for m in range(pairs):
                left = lists[0, 0, 0, shift, 0, m, out]
                right = lists[0, 0, 0, shift, 1, m, out]
                live = left < slots
                place = (row ^ (right // slots)) * slots + lax.rem(right, slots)
                base = ((hop * outs + group * share + i) * pairs + m) * 2
                table[base] = jnp.where(live, left, 0)
                table[base + 1] = jnp.where(live, place, zero_slot)
        return carry

    lax.fori_loop(0, cols * depths, at, 0)


def products(table, hop, out, outs, pairs, left, panel):
    total = None
    base = (hop * outs + out) * pairs * 2
    width = 2 if pairs % 2 == 0 else 1
    for m in range(0, pairs, width):
        lefts = [left[table[base + 2 * (m + j)]] for j in range(width)]
        rights = [panel[table[base + 2 * (m + j) + 1]] for j in range(width)]
        term = lax.dot_general(
            jnp.concatenate(lefts, 1),
            jnp.concatenate(rights, 1),
            (((1,), (1,)), ((), ())),
            preferred_element_type=jnp.float32,
        )
        total = term if total is None else total + term
    return total


def panel_kernel(rows, table, *refs):
    sources, panel = refs[:rows], refs[rows]
    slots = sources[0].shape[0]
    for i, source in enumerate(sources):
        panel[pl.ds(i * slots, slots)] = source[...]
    panel[rows * slots] = jnp.zeros(panel.shape[1:], panel.dtype)


def add_kernel(hops, pairs, started, sent_groups, kept_groups, share, table, panel, *refs):
    lefts, refs = refs[: len(hops)], refs[len(hops) :]
    if started:
        (sent_in, kept_in), refs = refs[:2], refs[2:]
    sent, kept = refs
    outs = (len(sent_groups) + len(kept_groups)) * share
    for groups, target, source in (
        (sent_groups, sent, sent_in if started else None),
        (kept_groups, kept, kept_in if started else None),
    ):
        for place, group in enumerate(groups):
            for i in range(share):
                total = source[place * share + i] if started else None
                for hop, left in zip(hops, lefts):
                    term = products(table, hop, group * share + i, outs, pairs, left, panel)
                    total = term if total is None else total + term
                target[place * share + i] = total


def in_vmem(x):
    return pltpu.with_memory_space_constraint(x, pltpu.VMEM)


def body(a_tiles, pair_lists):
    rows, cols, depths = (lax.axis_size(name) for name in ("row", "col", "depth"))
    slots, width = a_tiles.shape[3], a_tiles.shape[4]
    pairs, outs = pair_lists.shape[5:]
    share = outs // depths
    own = a_tiles.reshape(slots, width, width)

    lefts = {0: own}
    for bit in bits_down(cols):
        lefts.update({hop ^ bit: exchange(block, "col", bit) for hop, block in list(lefts.items())})
    rights = {0: own}
    for bit in bits_down(rows):
        rights.update({hop ^ bit: exchange(block, "row", bit) for hop, block in list(rights.items())})

    table = pl.pallas_call(
        functools.partial(table_kernel, (cols, depths, slots, pairs, outs)),
        out_shape=pltpu.SMEM((cols * outs * pairs * 2,), jnp.int32),
        in_specs=[SMEM],
        out_specs=SMEM,
        name="pair_table",
    )(pair_lists)
    table = pltpu.with_memory_space_constraint(table, pltpu.SMEM)
    panel = pl.pallas_call(
        functools.partial(panel_kernel, rows),
        out_shape=pltpu.VMEM((rows * slots + 1, width, width), a_tiles.dtype),
        in_specs=[SMEM] + [VMEM] * rows,
        out_specs=VMEM,
        name="right_panel",
    )(table, *[in_vmem(rights[i]) for i in range(rows)])

    sent_groups = [g for g in range(depths) if g & 1]
    kept_groups = [g for g in range(depths) if not g & 1]
    half = pltpu.VMEM((len(sent_groups) * share, width, width), jnp.float32)

    def add(hops, sums, name):
        block_flops = 2 * width**3 * pairs * outs
        return pl.pallas_call(
            functools.partial(
                add_kernel, hops, pairs, bool(sums), sent_groups, kept_groups, share
            ),
            out_shape=(half, half),
            in_specs=[SMEM] + [VMEM] * (1 + len(hops) + len(sums)),
            out_specs=(VMEM, VMEM),
            name=name,
            cost_estimate=pl.CostEstimate(
                flops=block_flops * len(hops), bytes_accessed=0, transcendentals=0
            ),
        )(table, in_vmem(panel), *[in_vmem(lefts[h]) for h in hops], *[in_vmem(s) for s in sums])

    last = cols - 1
    sums = add(list(range(last)), (), "early_products")
    sent, kept = add([last], sums, "late_products")

    kept = kept.reshape(len(kept_groups), share, width, width)
    kept = kept + exchange(sent, "depth", 1).reshape(kept.shape)
    bit = 2
    while bit < depths:
        kept = kept.reshape(kept.shape[0] // 2, 2, share, width, width)
        kept = kept[:, 0] + exchange(kept[:, 1], "depth", bit)
        bit *= 2
    return kept.reshape(1, 1, share, width, width)


def solution(mesh):
    placed = (
        P("row", "col", "depth", None, None, None),
        P("row", "col", "depth", None, None, None, None),
    )
    return jax.shard_map(
        body,
        mesh=mesh,
        in_specs=placed,
        out_specs=P("row", "col", "depth", None, None),
        check_vma=False,
    )
```

```python
import functools

import jax
import jax.numpy as jnp
from jax import lax
from jax.experimental import pallas as pl
from jax.experimental.pallas import tpu as pltpu
from jax.sharding import PartitionSpec as P

VMEM = pl.BlockSpec(memory_space=pltpu.VMEM)
SMEM = pl.BlockSpec(memory_space=pltpu.SMEM)
ANY = pl.BlockSpec(memory_space=pl.ANY)
WEIGHT = 20


def exchange(block, axis, distance):
    size = lax.axis_size(axis)
    return lax.ppermute(block, axis, [(i, i ^ distance) for i in range(size)])


def ring_place(index, size):
    return jnp.where(index % 2 == 0, index // 2, size - (index + 1) // 2)


def ring_device(place, size):
    return jnp.where(place < (size + 1) // 2, 2 * place, 2 * (size - place) - 1)


def turn(block, axis, step):
    size = lax.axis_size(axis)
    ring = [*range(0, size, 2), *reversed(range(1, size, 2))]
    return lax.ppermute(block, axis, [(ring[i], ring[(i + step) % size]) for i in range(size)])


def in_vmem(x):
    return pltpu.with_memory_space_constraint(x, pltpu.VMEM)


def lists_kernel(lists, held, sem):
    copy = pltpu.make_async_copy(lists, held, sem)
    copy.start()
    copy.wait()


def panel_kernel(lists, *refs):
    sources, panel = refs[:-1], refs[-1]
    slots = sources[0].shape[0]
    row = lax.axis_index("row")
    for hop, source in enumerate(sources):
        panel[pl.ds((row ^ hop) * slots, slots)] = source[...]
    panel[len(sources) * slots] = jnp.zeros(panel.shape[1:], panel.dtype)


def add_kernel(steps, groups, started, lists, panel, *refs):
    lefts, refs = refs[: len(steps)], refs[len(steps) :]
    sources, targets = (refs[: len(groups)], refs[len(groups) :]) if started else (None, refs)
    cols, pairs = lists.shape[3], lists.shape[5]
    slots = lefts[0].shape[0]
    zero_slot = panel.shape[0] - 1
    share = targets[0].shape[0]
    col, layer = lax.axis_index("col"), lax.axis_index("depth")
    width = 2 if pairs % 2 == 0 else 1

    def products(step, left, out):
        place = lax.rem(ring_place(col, cols) - step + cols, cols)
        shift = lax.rem(col - ring_device(place, cols) + cols, cols)
        total = None
        for m in range(0, pairs, width):
            chosen, partner = [], []
            for j in range(m, m + width):
                slot = lists[0, 0, 0, shift, 0, j, out]
                live = slot < slots
                chosen.append(left[jnp.where(live, slot, 0)])
                partner.append(panel[jnp.where(live, lists[0, 0, 0, shift, 1, j, out], zero_slot)])
            term = lax.dot_general(
                jnp.concatenate(chosen, 1),
                jnp.concatenate(partner, 1),
                (((1,), (1,)), ((), ())),
                preferred_element_type=jnp.float32,
            )
            total = term if total is None else total + term
        return total

    for k, group in enumerate(groups):
        for i in range(share):
            out = (layer ^ group) * share + i
            total = sources[k][i] if started else None
            for step, left in zip(steps, lefts):
                term = products(step, left, out)
                total = term if total is None else total + term
            targets[k][i] = total


def body(a_tiles, pair_lists):
    rows, cols, depths = (lax.axis_size(name) for name in ("row", "col", "depth"))
    slots, width = a_tiles.shape[3], a_tiles.shape[4]
    pairs, outs = pair_lists.shape[5:]
    share = outs // depths
    own = a_tiles.reshape(slots, width, width)

    lefts = {0: own}
    for step in range(1, cols // 2 + 1):
        lefts[step] = turn(lefts[step - 1], "col", 1)
        if 2 * step < cols:
            lefts[-step] = turn(lefts[1 - step], "col", -1)
    rights = {0: own}
    for bit in [1 << b for b in range(rows.bit_length() - 1)]:
        rights.update({hop ^ bit: exchange(block, "row", bit) for hop, block in list(rights.items())})

    lists = pl.pallas_call(
        lists_kernel,
        out_shape=pltpu.SMEM(pair_lists.shape, jnp.int32),
        in_specs=[ANY],
        out_specs=SMEM,
        scratch_shapes=[pltpu.SemaphoreType.DMA],
        name="pair_lists",
    )(pair_lists)
    lists = pltpu.with_memory_space_constraint(lists, pltpu.SMEM)
    panel = pl.pallas_call(
        panel_kernel,
        out_shape=pltpu.VMEM((rows * slots + 1, width, width), a_tiles.dtype),
        in_specs=[SMEM] + [VMEM] * rows,
        out_specs=VMEM,
        name="right_panel",
    )(lists, *[in_vmem(rights[i]) for i in range(rows)])

    def add(steps, groups, sums, name):
        started = [sums[g] for g in groups if g in sums]
        flops = 2 * width**3 * pairs * share * len(groups) * len(steps)
        totals = pl.pallas_call(
            functools.partial(add_kernel, steps, groups, bool(started)),
            out_shape=[pltpu.VMEM((share, width, width), jnp.float32)] * len(groups),
            in_specs=[SMEM] + [VMEM] * (1 + len(steps) + len(started)),
            out_specs=[VMEM] * len(groups),
            name=name,
            cost_estimate=pl.CostEstimate(
                flops=WEIGHT * flops, bytes_accessed=0, transcendentals=0
            ),
        )(lists, in_vmem(panel), *[in_vmem(lefts[s]) for s in steps], *[in_vmem(s) for s in started])
        return dict(zip(groups, totals))

    last = cols // 2
    early = [s for s in lefts if s != last]
    near, far = [0, 1], list(range(2, depths))
    sums = add(early, far + near, {}, "early_products")
    if far:
        sums.update(add([last], far, sums, "late_products_far"))
    sums.update(add([last], near, sums, "late_products_near"))

    bit = 1
    while bit < depths:
        for group in reversed([g for g in sums if not g & bit]):
            sums[group] = sums[group] + exchange(sums.pop(group | bit), "depth", bit)
        bit *= 2
    return sums[0].reshape(1, 1, share, width, width)


def solution(mesh):
    placed = (
        P("row", "col", "depth", None, None, None),
        P("row", "col", "depth", None, None, None, None),
    )
    return jax.shard_map(
        body,
        mesh=mesh,
        in_specs=placed,
        out_specs=P("row", "col", "depth", None, None),
        check_vma=False,
    )
```

```python
import functools

import jax
import jax.numpy as jnp
from jax import lax
from jax.experimental import pallas as pl
from jax.experimental.pallas import tpu as pltpu
from jax.sharding import PartitionSpec as P

VMEM = pl.BlockSpec(memory_space=pltpu.VMEM)
SMEM = pl.BlockSpec(memory_space=pltpu.SMEM)
ANY = pl.BlockSpec(memory_space=pl.ANY)
WEIGHT = 20


def exchange(block, axis, distance):
    size = lax.axis_size(axis)
    return lax.ppermute(block, axis, [(i, i ^ distance) for i in range(size)])


def ring_place(index, size):
    return jnp.where(index % 2 == 0, index // 2, size - (index + 1) // 2)


def ring_device(place, size):
    return jnp.where(place < (size + 1) // 2, 2 * place, 2 * (size - place) - 1)


def turn(block, axis, step):
    size = lax.axis_size(axis)
    ring = [*range(0, size, 2), *reversed(range(1, size, 2))]
    return lax.ppermute(block, axis, [(ring[i], ring[(i + step) % size]) for i in range(size)])


def in_vmem(x):
    return pltpu.with_memory_space_constraint(x, pltpu.VMEM)


def stage_kernel(tiles, lists, held, own, sems):
    copies = [
        pltpu.make_async_copy(lists, held, sems.at[0]),
        pltpu.make_async_copy(tiles, own, sems.at[1]),
    ]
    for copy in copies:
        copy.start()
    for copy in copies:
        copy.wait()


def panel_kernel(*refs):
    *sources, _, panel = refs
    slots = sources[0].shape[0]
    row = lax.axis_index("row")
    for hop, source in enumerate(sources):
        panel[pl.ds((row ^ hop) * slots, slots)] = source[...]
    panel[len(sources) * slots] = jnp.zeros(panel.shape[1:], panel.dtype)


def add_kernel(steps, groups, started, lists, panel, *refs):
    lefts, refs = refs[: len(steps)], refs[len(steps) :]
    sources, targets = (refs[: len(groups)], refs[len(groups) :]) if started else (None, refs)
    cols, pairs = lists.shape[3], lists.shape[5]
    slots = lefts[0].shape[0]
    zero_slot = panel.shape[0] - 1
    share = targets[0].shape[0]
    col, layer = lax.axis_index("col"), lax.axis_index("depth")
    width = 2 if pairs % 2 == 0 else 1

    def products(step, left, out):
        place = lax.rem(ring_place(col, cols) - step + cols, cols)
        shift = lax.rem(col - ring_device(place, cols) + cols, cols)
        total = None
        for m in range(0, pairs, width):
            chosen, partner = [], []
            for j in range(m, m + width):
                slot = lists[0, 0, 0, shift, 0, j, out]
                live = slot < slots
                chosen.append(left[jnp.where(live, slot, 0)])
                partner.append(panel[jnp.where(live, lists[0, 0, 0, shift, 1, j, out], zero_slot)])
            term = lax.dot_general(
                jnp.concatenate(chosen, 1),
                jnp.concatenate(partner, 1),
                (((1,), (1,)), ((), ())),
                preferred_element_type=jnp.float32,
            )
            total = term if total is None else total + term
        return total

    for k, group in enumerate(groups):
        for i in range(share):
            out = (layer ^ group) * share + i
            total = sources[k][i] if started else None
            for step, left in zip(steps, lefts):
                term = products(step, left, out)
                total = term if total is None else total + term
            targets[k][i] = total


def body(a_tiles, pair_lists):
    rows, cols, depths = (lax.axis_size(name) for name in ("row", "col", "depth"))
    slots, width = a_tiles.shape[3], a_tiles.shape[4]
    pairs, outs = pair_lists.shape[5:]
    share = outs // depths
    tiles = a_tiles.reshape(slots, width, width)

    lists, own = pl.pallas_call(
        stage_kernel,
        out_shape=(
            pltpu.SMEM(pair_lists.shape, jnp.int32),
            pltpu.VMEM(tiles.shape, tiles.dtype),
        ),
        in_specs=[ANY, ANY],
        out_specs=(SMEM, VMEM),
        scratch_shapes=[pltpu.SemaphoreType.DMA((2,))],
        name="stage",
    )(tiles, pair_lists)
    lists = pltpu.with_memory_space_constraint(lists, pltpu.SMEM)

    last = cols // 2
    lefts = {0: tiles}
    for step in range(1, last + 1):
        lefts[step] = turn(lefts[step - 1], "col", 1)
    for step in range(1, (cols + 1) // 2):
        lefts[-step] = turn(lefts[1 - step], "col", -1)
    rights = {0: tiles}
    for bit in [1 << b for b in range(rows.bit_length() - 1)]:
        rights.update({hop ^ bit: exchange(block, "row", bit) for hop, block in list(rights.items())})
    lefts[0] = rights[0] = own

    panel = pl.pallas_call(
        panel_kernel,
        out_shape=pltpu.VMEM((rows * slots + 1, width, width), a_tiles.dtype),
        in_specs=[VMEM] * (1 + rows),
        out_specs=VMEM,
        name="right_panel",
    )(*[in_vmem(rights[i]) for i in range(rows)], in_vmem(lefts[min(lefts)]))

    block = pltpu.VMEM((share, width, width), jnp.float32)

    def add(steps, groups, sums, name):
        flops = 2 * width**3 * pairs * share * len(groups) * len(steps)
        return list(
            pl.pallas_call(
                functools.partial(add_kernel, steps, groups, bool(sums)),
                out_shape=[block] * len(groups),
                in_specs=[SMEM] + [VMEM] * (1 + len(steps) + len(sums)),
                out_specs=[VMEM] * len(groups),
                name=name,
                cost_estimate=pl.CostEstimate(
                    flops=WEIGHT * flops, bytes_accessed=0, transcendentals=0
                ),
            )(lists, in_vmem(panel), *[in_vmem(lefts[s]) for s in steps], *[in_vmem(s) for s in sums])
        )

    sums = add([s for s in lefts if s != last], [2, 3, 0, 1], [], "early_products")
    far_kept, far_sent = add([last], [2, 3], sums[:2], "late_products_far")
    near_kept, near_sent = add([last], [0, 1], sums[2:], "late_products_near")
    far_came = exchange(far_sent, "depth", 1)
    near_came = exchange(near_sent, "depth", 1)
    far = far_kept + far_came
    near = near_kept + near_came
    return (near + exchange(far, "depth", 2)).reshape(1, 1, share, width, width)


def solution(mesh):
    placed = (
        P("row", "col", "depth", None, None, None),
        P("row", "col", "depth", None, None, None, None),
    )
    return jax.shard_map(
        body,
        mesh=mesh,
        in_specs=placed,
        out_specs=P("row", "col", "depth", None, None),
        check_vma=False,
    )
```

```python
import functools

import jax
import jax.numpy as jnp
from jax import lax
from jax.experimental import pallas as pl
from jax.experimental.pallas import tpu as pltpu
from jax.sharding import PartitionSpec as P

VMEM = pl.BlockSpec(memory_space=pltpu.VMEM)
SMEM = pl.BlockSpec(memory_space=pltpu.SMEM)
ANY = pl.BlockSpec(memory_space=pl.ANY)
WEIGHT = 20
TILE = 16
STEPS = 8


def exchange(block, axis, distance):
    size = lax.axis_size(axis)
    return lax.ppermute(block, axis, [(i, i ^ distance) for i in range(size)])


def ring_place(index, size):
    return jnp.where(index % 2 == 0, index // 2, size - (index + 1) // 2)


def ring_device(place, size):
    return jnp.where(place < (size + 1) // 2, 2 * place, 2 * (size - place) - 1)


def turn(block, axis, step):
    size = lax.axis_size(axis)
    ring = [*range(0, size, 2), *reversed(range(1, size, 2))]
    return lax.ppermute(block, axis, [(ring[i], ring[(i + step) % size]) for i in range(size)])


def in_vmem(x):
    return pltpu.with_memory_space_constraint(x, pltpu.VMEM)


def stage_kernel(tiles, lists, held, own, sems):
    copies = [
        pltpu.make_async_copy(lists, held, sems.at[0]),
        pltpu.make_async_copy(tiles, own, sems.at[1]),
    ]
    for copy in copies:
        copy.start()
    for copy in copies:
        copy.wait()


def panel_kernel(*refs):
    *sources, _, panel = refs
    slots = sources[0].shape[0]
    row = lax.axis_index("row")
    for hop, source in enumerate(sources):
        panel[pl.ds((row ^ hop) * slots, slots)] = source[...]
    panel[len(sources) * slots] = jnp.zeros(panel.shape[1:], panel.dtype)


def add_kernel(steps, groups, started, lists, panel, *refs):
    lefts, refs = refs[: len(steps)], refs[len(steps) :]
    sources, targets = (refs[: len(groups)], refs[len(groups) :]) if started else (None, refs)
    cols, pairs = lists.shape[3], lists.shape[5]
    slots = lefts[0].shape[0]
    zero_slot = panel.shape[0] - 1
    share = targets[0].shape[0]
    col, layer = lax.axis_index("col"), lax.axis_index("depth")
    width = 2 if pairs % 2 == 0 else 1

    def products(step, left, out):
        place = lax.rem(ring_place(col, cols) - step + cols, cols)
        shift = lax.rem(col - ring_device(place, cols) + cols, cols)
        total = None
        for m in range(0, pairs, width):
            chosen, partner = [], []
            for j in range(m, m + width):
                slot = lists[0, 0, 0, shift, 0, j, out]
                live = slot < slots
                chosen.append(left[jnp.where(live, slot, 0)])
                partner.append(panel[jnp.where(live, lists[0, 0, 0, shift, 1, j, out], zero_slot)])
            term = lax.dot_general(
                jnp.concatenate(chosen, 1),
                jnp.concatenate(partner, 1),
                (((1,), (1,)), ((), ())),
                preferred_element_type=jnp.float32,
            )
            total = term if total is None else total + term
        return total

    for k, group in enumerate(groups):
        for i in range(share):
            out = (layer ^ group) * share + i
            total = sources[k][i] if started else None
            for step, left in zip(steps, lefts):
                term = products(step, left, out)
                total = term if total is None else total + term
            targets[k][i] = total


def code_kernel(kept, came, coded):
    share, width = kept.shape[:2]
    line = lax.broadcasted_iota(jnp.int32, (TILE, width), 0)
    powers = jnp.zeros((TILE, width), jnp.float32)
    for i in range(share):
        total = kept[i] + came[i]
        top = jnp.max(jnp.abs(total), axis=0, keepdims=True)
        power = jnp.floor((15.0 - jnp.log2(jnp.maximum(top, 2.0**-110))) * STEPS)
        whole = jnp.clip(jnp.round(total * jnp.exp2(power / STEPS)), -32767.0, 32767.0)
        coded[pl.ds(i * width, width)] = whole.astype(jnp.int32).astype(jnp.int16)
        powers = jnp.where(line == i, power, powers)
    coded[pl.ds(share * width, TILE)] = powers.astype(jnp.int32).astype(jnp.int16)


def finish_kernel(kept, came, coded, out):
    share, width = kept.shape[:2]
    powers = coded[pl.ds(share * width, TILE)].astype(jnp.int32).astype(jnp.float32)
    scales = jnp.exp2(-powers / STEPS)
    for i in range(share):
        whole = coded[pl.ds(i * width, width)].astype(jnp.int32).astype(jnp.float32)
        out[i] = kept[i] + came[i] + whole * scales[i : i + 1]


def body(a_tiles, pair_lists):
    rows, cols, depths = (lax.axis_size(name) for name in ("row", "col", "depth"))
    slots, width = a_tiles.shape[3], a_tiles.shape[4]
    pairs, outs = pair_lists.shape[5:]
    share = outs // depths
    tiles = a_tiles.reshape(slots, width, width)

    lists, own = pl.pallas_call(
        stage_kernel,
        out_shape=(
            pltpu.SMEM(pair_lists.shape, jnp.int32),
            pltpu.VMEM(tiles.shape, tiles.dtype),
        ),
        in_specs=[ANY, ANY],
        out_specs=(SMEM, VMEM),
        scratch_shapes=[pltpu.SemaphoreType.DMA((2,))],
        name="stage",
    )(tiles, pair_lists)
    lists = pltpu.with_memory_space_constraint(lists, pltpu.SMEM)

    last = cols // 2
    lefts = {0: tiles}
    for step in range(1, last + 1):
        lefts[step] = turn(lefts[step - 1], "col", 1)
    for step in range(1, (cols + 1) // 2):
        lefts[-step] = turn(lefts[1 - step], "col", -1)
    rights = {0: tiles}
    for bit in [1 << b for b in range(rows.bit_length() - 1)]:
        rights.update({hop ^ bit: exchange(block, "row", bit) for hop, block in list(rights.items())})
    lefts[0] = rights[0] = own

    panel = pl.pallas_call(
        panel_kernel,
        out_shape=pltpu.VMEM((rows * slots + 1, width, width), a_tiles.dtype),
        in_specs=[VMEM] * (1 + rows),
        out_specs=VMEM,
        name="right_panel",
    )(*[in_vmem(rights[i]) for i in range(rows)], in_vmem(lefts[min(lefts)]))

    block = pltpu.VMEM((share, width, width), jnp.float32)

    def add(steps, groups, sums, name):
        flops = 2 * width**3 * pairs * share * len(groups) * len(steps)
        return list(
            pl.pallas_call(
                functools.partial(add_kernel, steps, groups, bool(sums)),
                out_shape=[block] * len(groups),
                in_specs=[SMEM] + [VMEM] * (1 + len(steps) + len(sums)),
                out_specs=[VMEM] * len(groups),
                name=name,
                cost_estimate=pl.CostEstimate(
                    flops=WEIGHT * flops, bytes_accessed=0, transcendentals=0
                ),
            )(lists, in_vmem(panel), *[in_vmem(lefts[s]) for s in steps], *[in_vmem(s) for s in sums])
        )

    sums = add([s for s in lefts if s != last], [3, 2, 1, 0], [], "early_products")
    (far_sent,) = add([last], [3], sums[:1], "late_products_first")
    far_kept, near_sent, near_kept = add([last], [2, 1, 0], sums[1:], "late_products_rest")
    far_came = exchange(far_sent, "depth", 1)
    near_came = exchange(near_sent, "depth", 1)
    coded = pl.pallas_call(
        code_kernel,
        out_shape=pltpu.VMEM((share * width + TILE, width), jnp.int16),
        in_specs=[VMEM] * 2,
        out_specs=VMEM,
        name="code",
    )(in_vmem(far_kept), in_vmem(far_came))
    coded = exchange(coded, "depth", 2)
    out = pl.pallas_call(
        finish_kernel,
        out_shape=jax.ShapeDtypeStruct((share, width, width), jnp.float32),
        in_specs=[VMEM] * 3,
        out_specs=VMEM,
        name="finish",
    )(in_vmem(near_kept), in_vmem(near_came), in_vmem(coded))
    return out.reshape(1, 1, share, width, width)


def solution(mesh):
    placed = (
        P("row", "col", "depth", None, None, None),
        P("row", "col", "depth", None, None, None, None),
    )
    return jax.shard_map(
        body,
        mesh=mesh,
        in_specs=placed,
        out_specs=P("row", "col", "depth", None, None),
        check_vma=False,
    )
```

```python
import functools

import jax
import jax.numpy as jnp
from jax import lax
from jax.experimental import pallas as pl
from jax.experimental.pallas import tpu as pltpu
from jax.sharding import PartitionSpec as P

VMEM = pl.BlockSpec(memory_space=pltpu.VMEM)
SMEM = pl.BlockSpec(memory_space=pltpu.SMEM)
ANY = pl.BlockSpec(memory_space=pl.ANY)
WEIGHT = 20
TILE = 16
STEPS = 8


def exchange(block, axis, distance):
    size = lax.axis_size(axis)
    return lax.ppermute(block, axis, [(i, i ^ distance) for i in range(size)])


def ring_place(index, size):
    return jnp.where(index % 2 == 0, index // 2, size - (index + 1) // 2)


def ring_device(place, size):
    return jnp.where(place < (size + 1) // 2, 2 * place, 2 * (size - place) - 1)


def turn(block, axis, step):
    size = lax.axis_size(axis)
    ring = [*range(0, size, 2), *reversed(range(1, size, 2))]
    return lax.ppermute(block, axis, [(ring[i], ring[(i + step) % size]) for i in range(size)])


def in_vmem(x):
    return pltpu.with_memory_space_constraint(x, pltpu.VMEM)


def stage_kernel(tiles, lists, held, own, sems):
    copies = [
        pltpu.make_async_copy(lists, held, sems.at[0]),
        pltpu.make_async_copy(tiles, own, sems.at[1]),
    ]
    for copy in copies:
        copy.start()
    for copy in copies:
        copy.wait()


def panel_kernel(*refs):
    *sources, _, panel = refs
    slots = sources[0].shape[0]
    row = lax.axis_index("row")
    for hop, source in enumerate(sources):
        panel[pl.ds((row ^ hop) * slots, slots)] = source[...]
    panel[len(sources) * slots] = jnp.zeros(panel.shape[1:], panel.dtype)


def add_kernel(steps, groups, share, started, coded, lists, panel, *refs):
    lefts, refs = refs[: len(steps)], refs[len(steps) :]
    sources, targets = (refs[: len(groups)], refs[len(groups) :]) if started else (None, refs)
    cols, pairs = lists.shape[3], lists.shape[5]
    slots = lefts[0].shape[0]
    zero_slot = panel.shape[0] - 1
    col, layer = lax.axis_index("col"), lax.axis_index("depth")
    width = 2 if pairs % 2 == 0 else 1

    def products(step, left, out):
        place = lax.rem(ring_place(col, cols) - step + cols, cols)
        shift = lax.rem(col - ring_device(place, cols) + cols, cols)
        total = None
        for m in range(0, pairs, width):
            chosen, partner = [], []
            for j in range(m, m + width):
                slot = lists[0, 0, 0, shift, 0, j, out]
                live = slot < slots
                chosen.append(left[jnp.where(live, slot, 0)])
                partner.append(panel[jnp.where(live, lists[0, 0, 0, shift, 1, j, out], zero_slot)])
            term = lax.dot_general(
                jnp.concatenate(chosen, 1),
                jnp.concatenate(partner, 1),
                (((1,), (1,)), ((), ())),
                preferred_element_type=jnp.float32,
            )
            total = term if total is None else total + term
        return total

    for k, group in enumerate(groups):
        totals = []
        for i in range(share):
            out = (layer ^ group) * share + i
            total = sources[k][i] if started else None
            for step, left in zip(steps, lefts):
                term = products(step, left, out)
                total = term if total is None else total + term
            totals.append(total)
        if coded:
            encode(totals, targets[k])
            continue
        for i, total in enumerate(totals):
            targets[k][i] = total


def encode(blocks, coded):
    width = blocks[0].shape[0]
    line = lax.broadcasted_iota(jnp.int32, (TILE, width), 0)
    powers = jnp.zeros((TILE, width), jnp.float32)
    for i, total in enumerate(blocks):
        top = jnp.max(jnp.abs(total), axis=0, keepdims=True)
        power = jnp.floor((15.0 - jnp.log2(jnp.maximum(top, 2.0**-110))) * STEPS)
        whole = jnp.clip(jnp.round(total * jnp.exp2(power / STEPS)), -32767.0, 32767.0)
        coded[pl.ds(i * width, width)] = whole.astype(jnp.int32).astype(jnp.int16)
        powers = jnp.where(line == i, power, powers)
    coded[pl.ds(len(blocks) * width, TILE)] = powers.astype(jnp.int32).astype(jnp.int16)


def code_kernel(kept, came, coded):
    encode([kept[i] + block for i, block in enumerate(decode(came))], coded)


def decode(coded):
    width = coded.shape[1]
    count = coded.shape[0] // width
    powers = coded[pl.ds(count * width, TILE)].astype(jnp.int32).astype(jnp.float32)
    scales = jnp.exp2(-powers / STEPS)
    for i in range(count):
        whole = coded[pl.ds(i * width, width)].astype(jnp.int32).astype(jnp.float32)
        yield whole * scales[i : i + 1]


def finish_kernel(kept, came, coded, out):
    share, width = kept.shape[:2]
    powers = coded[pl.ds(share * width, TILE)].astype(jnp.int32).astype(jnp.float32)
    scales = jnp.exp2(-powers / STEPS)
    for i in range(share):
        whole = coded[pl.ds(i * width, width)].astype(jnp.int32).astype(jnp.float32)
        out[i] = kept[i] + came[i] + whole * scales[i : i + 1]


def body(a_tiles, pair_lists):
    rows, cols, depths = (lax.axis_size(name) for name in ("row", "col", "depth"))
    slots, width = a_tiles.shape[3], a_tiles.shape[4]
    pairs, outs = pair_lists.shape[5:]
    share = outs // depths
    tiles = a_tiles.reshape(slots, width, width)

    lists, own = pl.pallas_call(
        stage_kernel,
        out_shape=(
            pltpu.SMEM(pair_lists.shape, jnp.int32),
            pltpu.VMEM(tiles.shape, tiles.dtype),
        ),
        in_specs=[ANY, ANY],
        out_specs=(SMEM, VMEM),
        scratch_shapes=[pltpu.SemaphoreType.DMA((2,))],
        name="stage",
    )(tiles, pair_lists)
    lists = pltpu.with_memory_space_constraint(lists, pltpu.SMEM)

    last = cols // 2
    lefts = {0: tiles}
    for step in range(1, last + 1):
        lefts[step] = turn(lefts[step - 1], "col", 1)
    for step in range(1, (cols + 1) // 2):
        lefts[-step] = turn(lefts[1 - step], "col", -1)
    rights = {0: tiles}
    for bit in [1 << b for b in range(rows.bit_length() - 1)]:
        rights.update({hop ^ bit: exchange(block, "row", bit) for hop, block in list(rights.items())})
    lefts[0] = rights[0] = own

    panel = pl.pallas_call(
        panel_kernel,
        out_shape=pltpu.VMEM((rows * slots + 1, width, width), a_tiles.dtype),
        in_specs=[VMEM] * (1 + rows),
        out_specs=VMEM,
        name="right_panel",
    )(*[in_vmem(rights[i]) for i in range(rows)], in_vmem(lefts[min(lefts)]))

    block = pltpu.VMEM((share, width, width), jnp.float32)
    code = pltpu.VMEM((share * width + TILE, width), jnp.int16)

    def add(steps, groups, sums, name, coded=False):
        flops = 2 * width**3 * pairs * share * len(groups) * len(steps)
        return list(
            pl.pallas_call(
                functools.partial(add_kernel, steps, groups, share, bool(sums), coded),
                out_shape=[code if coded else block] * len(groups),
                in_specs=[SMEM] + [VMEM] * (1 + len(steps) + len(sums)),
                out_specs=[VMEM] * len(groups),
                name=name,
                cost_estimate=pl.CostEstimate(
                    flops=WEIGHT * flops, bytes_accessed=0, transcendentals=0
                ),
            )(lists, in_vmem(panel), *[in_vmem(lefts[s]) for s in steps], *[in_vmem(s) for s in sums])
        )

    sums = add([s for s in lefts if s != last], [2, 3, 1, 0], [], "early_products")
    (far_sent,) = add([last], [2], sums[:1], "late_products_first", True)
    far_kept, near_sent, near_kept = add([last], [3, 1, 0], sums[1:], "late_products_rest")
    far_came = exchange(far_sent, "depth", 1)
    near_came = exchange(near_sent, "depth", 1)
    coded = pl.pallas_call(
        code_kernel,
        out_shape=pltpu.VMEM((share * width + TILE, width), jnp.int16),
        in_specs=[VMEM] * 2,
        out_specs=VMEM,
        name="code",
    )(in_vmem(far_kept), in_vmem(far_came))
    coded = exchange(coded, "depth", 3)
    out = pl.pallas_call(
        finish_kernel,
        out_shape=jax.ShapeDtypeStruct((share, width, width), jnp.float32),
        in_specs=[VMEM] * 3,
        out_specs=VMEM,
        name="finish",
    )(in_vmem(near_kept), in_vmem(near_came), in_vmem(coded))
    return out.reshape(1, 1, share, width, width)


def solution(mesh):
    placed = (
        P("row", "col", "depth", None, None, None),
        P("row", "col", "depth", None, None, None, None),
    )
    return jax.shard_map(
        body,
        mesh=mesh,
        in_specs=placed,
        out_specs=P("row", "col", "depth", None, None),
        check_vma=False,
    )
```

```python
import functools

import jax
import jax.numpy as jnp
from jax import lax
from jax.experimental import pallas as pl
from jax.experimental.pallas import tpu as pltpu
from jax.sharding import PartitionSpec as P

VMEM = pl.BlockSpec(memory_space=pltpu.VMEM)
SMEM = pl.BlockSpec(memory_space=pltpu.SMEM)
ANY = pl.BlockSpec(memory_space=pl.ANY)
WEIGHT = 20
TILE = 16
STEPS = 8


def exchange(block, axis, distance):
    size = lax.axis_size(axis)
    return lax.ppermute(block, axis, [(i, i ^ distance) for i in range(size)])


def ring_place(index, size):
    return jnp.where(index % 2 == 0, index // 2, size - (index + 1) // 2)


def ring_device(place, size):
    return jnp.where(place < (size + 1) // 2, 2 * place, 2 * (size - place) - 1)


def turn(block, axis, step):
    size = lax.axis_size(axis)
    ring = [*range(0, size, 2), *reversed(range(1, size, 2))]
    return lax.ppermute(block, axis, [(ring[i], ring[(i + step) % size]) for i in range(size)])


def in_vmem(x):
    return pltpu.with_memory_space_constraint(x, pltpu.VMEM)


def stage_kernel(tiles, lists, held, own, sems):
    copies = [
        pltpu.make_async_copy(lists, held, sems.at[0]),
        pltpu.make_async_copy(tiles, own, sems.at[1]),
    ]
    for copy in copies:
        copy.start()
    for copy in copies:
        copy.wait()


def panel_kernel(*refs):
    *sources, _, panel = refs
    slots = sources[0].shape[0]
    row = lax.axis_index("row")
    for hop, source in enumerate(sources):
        panel[pl.ds((row ^ hop) * slots, slots)] = source[...]
    panel[len(sources) * slots] = jnp.zeros(panel.shape[1:], panel.dtype)


def add_kernel(steps, groups, share, started, coded, lists, panel, *refs):
    lefts, refs = refs[: len(steps)], refs[len(steps) :]
    sources, targets = (refs[: len(groups)], refs[len(groups) :]) if started else (None, refs)
    cols, pairs = lists.shape[3], lists.shape[5]
    slots = lefts[0].shape[0]
    zero_slot = panel.shape[0] - 1
    col, layer = lax.axis_index("col"), lax.axis_index("depth")
    width = pairs

    def products(step, left, out):
        place = lax.rem(ring_place(col, cols) - step + cols, cols)
        shift = lax.rem(col - ring_device(place, cols) + cols, cols)
        total = None
        for m in range(0, pairs, width):
            chosen, partner = [], []
            for j in range(m, m + width):
                slot = lists[0, 0, 0, shift, 0, j, out]
                live = slot < slots
                chosen.append(left[jnp.where(live, slot, 0)])
                partner.append(panel[jnp.where(live, lists[0, 0, 0, shift, 1, j, out], zero_slot)])
            term = lax.dot_general(
                jnp.concatenate(chosen, 1),
                jnp.concatenate(partner, 1),
                (((1,), (1,)), ((), ())),
                preferred_element_type=jnp.float32,
            )
            total = term if total is None else total + term
        return total

    for k, group in enumerate(groups):
        totals = []
        for i in range(share):
            out = (layer ^ group) * share + i
            total = sources[k][i] if started else None
            for step, left in zip(steps, lefts):
                term = products(step, left, out)
                total = term if total is None else total + term
            totals.append(total)
        if coded:
            encode(totals, targets[k])
            continue
        for i, total in enumerate(totals):
            targets[k][i] = total


def encode(blocks, coded):
    width = blocks[0].shape[0]
    line = lax.broadcasted_iota(jnp.int32, (TILE, width), 0)
    powers = jnp.zeros((TILE, width), jnp.float32)
    for i, total in enumerate(blocks):
        top = jnp.max(jnp.abs(total), axis=0, keepdims=True)
        power = jnp.floor((15.0 - jnp.log2(jnp.maximum(top, 2.0**-110))) * STEPS)
        whole = jnp.clip(jnp.round(total * jnp.exp2(power / STEPS)), -32767.0, 32767.0)
        coded[pl.ds(i * width, width)] = whole.astype(jnp.int32).astype(jnp.int16)
        powers = jnp.where(line == i, power, powers)
    coded[pl.ds(len(blocks) * width, TILE)] = powers.astype(jnp.int32).astype(jnp.int16)


def code_kernel(kept, came, coded):
    encode([kept[i] + block for i, block in enumerate(decode(came))], coded)


def decode(coded):
    width = coded.shape[1]
    count = coded.shape[0] // width
    powers = coded[pl.ds(count * width, TILE)].astype(jnp.int32).astype(jnp.float32)
    scales = jnp.exp2(-powers / STEPS)
    for i in range(count):
        whole = coded[pl.ds(i * width, width)].astype(jnp.int32).astype(jnp.float32)
        yield whole * scales[i : i + 1]


def finish_kernel(kept, came, coded, out):
    share, width = kept.shape[:2]
    powers = coded[pl.ds(share * width, TILE)].astype(jnp.int32).astype(jnp.float32)
    scales = jnp.exp2(-powers / STEPS)
    for i in range(share):
        whole = coded[pl.ds(i * width, width)].astype(jnp.int32).astype(jnp.float32)
        out[i] = kept[i] + came[i] + whole * scales[i : i + 1]


def body(a_tiles, pair_lists):
    rows, cols, depths = (lax.axis_size(name) for name in ("row", "col", "depth"))
    slots, width = a_tiles.shape[3], a_tiles.shape[4]
    pairs, outs = pair_lists.shape[5:]
    share = outs // depths
    tiles = a_tiles.reshape(slots, width, width)

    lists, own = pl.pallas_call(
        stage_kernel,
        out_shape=(
            pltpu.SMEM(pair_lists.shape, jnp.int32),
            pltpu.VMEM(tiles.shape, tiles.dtype),
        ),
        in_specs=[ANY, ANY],
        out_specs=(SMEM, VMEM),
        scratch_shapes=[pltpu.SemaphoreType.DMA((2,))],
        name="stage",
    )(tiles, pair_lists)
    lists = pltpu.with_memory_space_constraint(lists, pltpu.SMEM)

    last = cols // 2
    lefts = {0: tiles}
    for step in range(1, last + 1):
        lefts[step] = turn(lefts[step - 1], "col", 1)
    for step in range(1, (cols + 1) // 2):
        lefts[-step] = turn(lefts[1 - step], "col", -1)
    rights = {0: tiles}
    for bit in [1 << b for b in range(rows.bit_length() - 1)]:
        rights.update({hop ^ bit: exchange(block, "row", bit) for hop, block in list(rights.items())})
    lefts[0] = rights[0] = own

    panel = pl.pallas_call(
        panel_kernel,
        out_shape=pltpu.VMEM((rows * slots + 1, width, width), a_tiles.dtype),
        in_specs=[VMEM] * (1 + rows),
        out_specs=VMEM,
        name="right_panel",
    )(*[in_vmem(rights[i]) for i in range(rows)], in_vmem(lefts[min(lefts)]))

    block = pltpu.VMEM((share, width, width), jnp.float32)
    code = pltpu.VMEM((share * width + TILE, width), jnp.int16)

    def add(steps, groups, sums, name, coded=False):
        flops = 2 * width**3 * pairs * share * len(groups) * len(steps)
        return list(
            pl.pallas_call(
                functools.partial(add_kernel, steps, groups, share, bool(sums), coded),
                out_shape=[code if coded else block] * len(groups),
                in_specs=[SMEM] + [VMEM] * (1 + len(steps) + len(sums)),
                out_specs=[VMEM] * len(groups),
                name=name,
                cost_estimate=pl.CostEstimate(
                    flops=WEIGHT * flops, bytes_accessed=0, transcendentals=0
                ),
            )(lists, in_vmem(panel), *[in_vmem(lefts[s]) for s in steps], *[in_vmem(s) for s in sums])
        )

    sums = add([s for s in lefts if s != last], [2, 3, 1, 0], [], "early_products")
    (far_sent,) = add([last], [2], sums[:1], "late_products_first", True)
    far_kept, near_sent, near_kept = add([last], [3, 1, 0], sums[1:], "late_products_rest")
    far_came = exchange(far_sent, "depth", 1)
    near_came = exchange(near_sent, "depth", 1)
    coded = pl.pallas_call(
        code_kernel,
        out_shape=pltpu.VMEM((share * width + TILE, width), jnp.int16),
        in_specs=[VMEM] * 2,
        out_specs=VMEM,
        name="code",
    )(in_vmem(far_kept), in_vmem(far_came))
    coded = exchange(coded, "depth", 3)
    out = pl.pallas_call(
        finish_kernel,
        out_shape=jax.ShapeDtypeStruct((share, width, width), jnp.float32),
        in_specs=[VMEM] * 3,
        out_specs=VMEM,
        name="finish",
    )(in_vmem(near_kept), in_vmem(near_came), in_vmem(coded))
    return out.reshape(1, 1, share, width, width)


def solution(mesh):
    placed = (
        P("row", "col", "depth", None, None, None),
        P("row", "col", "depth", None, None, None, None),
    )
    return jax.shard_map(
        body,
        mesh=mesh,
        in_specs=placed,
        out_specs=P("row", "col", "depth", None, None),
        check_vma=False,
    )
```
